32 devices in a mesh: row: 8 (over z, y), col: 4 (over x, core).
Axes of the slice: x: 2, y: 2, z: 4, core: 2. Of those that a mesh axis runs over, the one named last changes fastest.
Arguments:
- coords: int32 [3, 4096], P(None, ('row', 'col')), may hold values from 0 to 5376, as said below
- mode_shapes: bfloat16 [256, 4096], P(None, ('row', 'col')), as said below
- output_shapes: bfloat16 [65536, 256], P(('row', 'col')), may hold values from -0.375 to 0.375
- response_gain: float32 [2, 256], replicated, may hold values from -4 to 4
Outputs:
- response_power: float32 [65536], P(('row', 'col'))
- modal_csd: float32 [256, 256], replicated
The draws below stay inside these ranges and needn't reach their ends.
Inputs may be any that keep to these rules, and one draw needn't show every extreme that they name: `coords`: positions of points on an aircraft's skin, numbered in no spatial order. `mode_shapes`: entries are of order 1 / sqrt(4096); each mode has a share of one sign over all nodes.
All inputs are finite; a program needn't handle non-finite values.
Results may differ from the reference program's by a relative error of at most 0.002.
Values may be sent and summed in bfloat16 or wider, within the bound.
No kernel may reach another device: no remote copies, remote signals or barrier semaphores. Data moves between devices by JAX's collectives and lax.ppermute only.
A program may use at most 64 MiB of HBM per device.

```python
import math
import jax
import jax.numpy as jnp
import numpy as np
from jax import lax

M = 256
NODES = 4096
CYCLE_NODES = 128
DOFS = 65536


def draw_mode_shapes(key, part):
    offset_key, noise_key = jax.random.split(key, 2)
    offset = jax.random.uniform(offset_key, (M, 1), jnp.float32, -0.5, 0.5)
    noise_draw = jnp.clip(jax.random.normal(noise_key, (M, NODES), jnp.float32), -4.0, 4.0)
    values = (offset + noise_draw) / jnp.sqrt(jnp.float32(NODES))
    return values.astype(jnp.bfloat16)


def draw_coords(key, part):
    cycle_size = CYCLE_NODES
    cycle_count = NODES // cycle_size
    fine_steps = 16
    step_count = cycle_size * fine_steps
    axial_pitch = 119
    angles = 2.0 * np.pi * np.arange(step_count) / step_count
    outline = 1.0 + 0.06 * np.cos(2.0 * angles) + 0.02 * np.cos(3.0 * angles)
    radius = axial_pitch * cycle_size / (2.0 * np.pi)
    across_table = np.floor(radius * outline * np.cos(angles) + 0.5).astype(np.int32)
    upward_table = np.floor(radius * outline * np.sin(angles) + 0.5).astype(np.int32)
    cycle_place = np.arange(cycle_count) / max(cycle_count - 1, 1)
    taper_shape = 1.0 - 0.25 * np.clip((cycle_place - 0.6) / 0.4, 0.0, 1.0) ** 2
    taper_table = np.floor(4096.0 * taper_shape + 0.5).astype(np.int32)
    offset_ticks = int(np.ceil(1.1 * radius))
    jitter_key, order_key = jax.random.split(key)
    node_index = jnp.arange(NODES, dtype=jnp.int32)
    frame_index = node_index // cycle_size
    slot_index = node_index - frame_index * cycle_size
    jitter = jax.random.randint(jitter_key, (NODES,), -5, 6, jnp.int32)
    position = (slot_index * fine_steps + jitter + step_count) % step_count
    taper_scale = jnp.asarray(taper_table)[frame_index]
    across_x = jnp.asarray(across_table)[position] * taper_scale // 4096 + offset_ticks
    across_y = jnp.asarray(upward_table)[position] * taper_scale // 4096 + offset_ticks
    axial_ticks = frame_index * axial_pitch
    placed = jnp.stack([across_x, across_y, axial_ticks]).astype(jnp.int32)
    node_order = jax.random.permutation(order_key, NODES)
    return placed[:, node_order]


def level_of(stream_key, dims, cuts, smallest, largest):
    loudness, own = 1.0, jax.random.fold_in(stream_key, 6)
    for dim, parts in cuts:
        steps = jnp.exp(jax.random.uniform(jax.random.fold_in(own, dim), (parts,), jnp.float32, smallest / len(cuts), largest / len(cuts)))
        loudness = loudness * jnp.repeat(steps, dims[dim] // parts).reshape([-1 if axis == dim else 1 for axis in range(len(dims))])
    return loudness


def bell_draw(key, shape, width, reach, cuts=(), kind=jnp.bfloat16):
    result = jax.random.normal(key, shape, jnp.float32) * width
    if len(cuts) > 0:
        result = level_of(key, shape, cuts, -0.22, 0.18) * result
    return jnp.clip(result, min=-reach, max=reach).astype(kind)


def setup_inputs(seed: int = 0) -> dict:
    key_list = jax.random.split(jax.random.key(seed), 5)
    coords = draw_coords(jax.random.fold_in(key_list[4], 71), 0)
    mode_shapes = draw_mode_shapes(jax.random.fold_in(key_list[4], 71), 0)
    output_shapes = bell_draw(key_list[2], (DOFS, M), M ** -0.5, 0.375, ((0, 32),))
    response_gain = bell_draw(key_list[3], (2, M), 1.0, 4.0, (), jnp.float32)
    return {"coords": coords, "mode_shapes": mode_shapes, "output_shapes": output_shapes, "response_gain": response_gain}


wave_scale = 0.35 / 64.0

def coherence(left_points, right_points):
    difference = (left_points[:, :, None] - right_points[:, None, :]).astype(jnp.float32)
    squared = lax.optimization_barrier(jnp.sum(difference * difference, axis=0))
    return jnp.sinc(wave_scale * jnp.sqrt(squared)).astype(jnp.bfloat16)

def reference(coords, mode_shapes, output_shapes, response_gain):
    node_total = coords.shape[1]
    mode_count = mode_shapes.shape[0]
    block_size = math.gcd(node_total, 512)
    block_count = node_total // block_size
    shapes_wide = mode_shapes.astype(jnp.float32)

    def one_block(block_start):
        block_points = lax.dynamic_slice_in_dim(coords, block_start, block_size, 1)
        coherence_tile = coherence(coords, block_points).astype(jnp.float32)
        return jnp.dot(shapes_wide, coherence_tile, precision=lax.Precision.HIGHEST)
    block_starts = (jnp.arange(block_count) * block_size).astype(jnp.int32)
    blocks = lax.map(one_block, block_starts)
    projection = jnp.transpose(blocks, (1, 0, 2)).reshape(mode_count, node_total)
    modal_csd = lax.dot_general(shapes_wide, projection, (((1,), (1,)), ((), ())), precision=lax.Precision.HIGHEST)
    real_part = response_gain[0]
    imag_part = response_gain[1]
    weighted = (real_part[:, None] * real_part[None, :] + imag_part[:, None] * imag_part[None, :]) * modal_csd
    outputs_wide = output_shapes.astype(jnp.float32)
    mapped = jnp.dot(outputs_wide, weighted, precision=lax.Precision.HIGHEST)
    response_power = lax.optimization_barrier(jnp.sum(mapped * outputs_wide, axis=1))
    return (response_power, modal_csd)
```

```python
import functools
import math

import jax
import jax.numpy as jnp
from jax import lax
from jax.experimental import pallas as pl
from jax.experimental.pallas import tpu as pltpu
from jax.sharding import PartitionSpec as P

wave_scale = 0.35 / 64.0
sine_terms = (
    0.9999999970821931,
    -0.6449338560287435,
    0.1668058873098644,
    -0.023932847910373648,
    0.0021836636774330933,
    -0.00012284698513521545,
)
period_shift = 1.5 * 2.0**24
axes = ("row", "col")
POINT_ROWS = 16


def coherence(left_points, right_points):
    difference = (left_points[:, :, None] - right_points[:, None, :]).astype(jnp.float32)
    squared = jnp.sum(difference * difference, axis=0)
    return jnp.sinc(wave_scale * jnp.sqrt(squared)).astype(jnp.bfloat16)


def split_parts(matrix):
    high_part = matrix.astype(jnp.bfloat16)
    low_part = (matrix - high_part.astype(jnp.float32)).astype(jnp.bfloat16)
    return (high_part, low_part)


def modal_product(node_shapes, node_projection):
    high_part, low_part = split_parts(node_projection)
    dims = (((1,), (1,)), ((), ()))
    upper = lax.dot_general(node_shapes, high_part, dims, preferred_element_type=jnp.float32)
    lower = lax.dot_general(node_shapes, low_part, dims, preferred_element_type=jnp.float32)
    return upper + lower


def local_general(coords, mode_shapes, output_shapes, response_gain):
    row_shapes = lax.all_gather(mode_shapes, "col", axis=1, tiled=True)
    row_points = lax.all_gather(coords, "col", axis=1, tiled=True)
    mode_count = mode_shapes.shape[0]
    piece_shapes = lax.all_gather(mode_shapes, "row", axis=1, tiled=True)
    piece_points = lax.all_gather(coords, "row", axis=1, tiled=True)
    length = piece_shapes.shape[1]
    block_size = math.gcd(length, 1024)

    def add_block(loop_index, running_sum):
        block_start = loop_index * block_size
        part_shapes = lax.dynamic_slice_in_dim(piece_shapes, block_start, block_size, 1)
        part_points = lax.dynamic_slice_in_dim(piece_points, block_start, block_size, 1)
        tile = coherence(part_points, row_points)
        return running_sum + jnp.dot(part_shapes, tile, preferred_element_type=jnp.float32)

    zero_block = jnp.zeros((mode_count, row_points.shape[1]), jnp.float32)
    projection = lax.fori_loop(0, length // block_size, add_block, zero_block)
    modal_csd = lax.psum(modal_product(row_shapes, projection), axes)
    real_part, imag_part = response_gain[0], response_gain[1]
    gains = real_part[:, None] * real_part[None, :] + imag_part[:, None] * imag_part[None, :]
    weighted_high, weighted_low = split_parts(gains * modal_csd)
    mapped = jnp.dot(output_shapes, weighted_high, preferred_element_type=jnp.float32)
    mapped = mapped + jnp.dot(output_shapes, weighted_low, preferred_element_type=jnp.float32)
    response_power = jnp.sum(mapped * output_shapes.astype(jnp.float32), axis=1)
    return (response_power, modal_csd)


BIT_X, BIT_Y, BIT_Z, BIT_W = 1, 2, 4, 8


def receive(array, source):
    count = lax.axis_size(axes)
    pairs = []
    for device in range(count):
        chip, core = source(device >> 1, device & 1)
        pairs.append((chip * 2 + core, device))
    return lax.ppermute(array, axes, pairs)


def other_core(array):
    return receive(array, lambda chip, core: (chip, 1 - core))


def left_points(block):
    rows = block[256 : 256 + POINT_ROWS, :].astype(jnp.float32)
    points = rows[0:8, :] * 256.0 + rows[8:16, :]
    columns = jnp.transpose(points, (1, 0))
    return [columns[:, k : k + 1] for k in range(3)]


def right_points(block):
    rows = block[256 : 256 + POINT_ROWS, :].astype(jnp.float32)
    points = rows[0:8, :] * 256.0 + rows[8:16, :]
    return [points[k : k + 1, :] for k in range(3)]


def coherence_tile(left, right):
    squared = None
    for left_column, right_row in zip(left, right):
        difference = left_column - right_row
        term = difference * difference
        squared = term if squared is None else squared + term
    squared = jnp.maximum(squared, 1e-6)
    inverse = lax.rsqrt(squared)
    x = squared * (inverse * wave_scale)
    r = x - ((x + period_shift) - period_shift)
    z = r * r
    scale = 1.0 / wave_scale
    q = jnp.full_like(z, sine_terms[-1] * scale)
    for term in sine_terms[-2::-1]:
        q = q * z + term * scale
    return ((r * (1.0 - z)) * (q * inverse)).astype(jnp.bfloat16)


def dot(a, b):
    return jnp.dot(a, b, preferred_element_type=jnp.float32)


def dot_t(a, b):
    return lax.dot_general(a, b, (((1,), (1,)), ((), ())), preferred_element_type=jnp.float32)


def beside(*arrays):
    return jnp.concatenate(arrays, axis=1)


def shapes_of(block):
    return block[0:256, :]


def quarter(left_block, right_block):
    tile = coherence_tile(left_points(left_block), right_points(right_block))
    return dot(shapes_of(left_block), tile).astype(jnp.bfloat16), shapes_of(right_block)


def full_pair(left_halves, right_halves):
    lefts = [left_points(h) for h in left_halves]
    rights = [right_points(h) for h in right_halves]
    shapes = beside(*[shapes_of(h) for h in left_halves])
    projections = []
    for right in rights:
        column = jnp.concatenate([coherence_tile(left, right) for left in lefts], axis=0)
        projections.append(dot(shapes, column).astype(jnp.bfloat16))
    return dot_t(beside(*projections), beside(*[shapes_of(h) for h in right_halves]))


def paired(jobs):
    projections, shapes = zip(*jobs)
    return dot_t(beside(*projections), beside(*shapes))


def early_kernel(own, a, e, c_own, c_other, bits, out):
    core = bits[0]
    mine = right_points(own[0])
    total = 0.5 * dot_t(
        dot(
            beside(shapes_of(own[0]), shapes_of(own[1])),
            jnp.concatenate(
                [coherence_tile(left_points(own[0]), mine), coherence_tile(left_points(own[1]), mine)], axis=0
            ),
        ).astype(jnp.bfloat16),
        shapes_of(own[0]),
    )
    u = bits[1]
    jobs = []
    for k in range(2):
        left_half, right_half = u * k, u | k
        jobs.append(quarter(own[left_half ^ core], a[right_half ^ core]))
    total += paired(jobs)
    u = bits[2]
    left_half = jnp.where(u == 1, 1, core)
    right_half = jnp.where(u == 1, core, 0)
    projection, shapes = quarter(e[left_half ^ (1 - core)], a[right_half ^ core])
    total += dot_t(projection, shapes)
    total += full_pair([a[0], a[1]], [c_own[...], c_other[...]])
    out[...] = total


def late_kernel(own, a, b, e, c_own, c_other, bits, early, out):
    core = bits[0]
    u = bits[3]
    total = early[...]
    jobs = []
    for k in range(2):
        left_half, right_half = u * k, u | k
        jobs.append(quarter(own[left_half ^ core], b[right_half ^ core]))
    total += paired(jobs)
    left_half = jnp.where(u == 1, 1, core)
    right_half = jnp.where(u == 1, core, 0)
    right = b[right_half ^ core]
    total += paired([quarter(a[left_half ^ core], right), quarter(e[left_half ^ (1 - core)], right)])
    total += full_pair([b[0], b[1]], [c_own[...], c_other[...]])
    first = total[0:128, 0:128] + total[0:128, 0:128].T
    second = total[128:256, 128:256] + total[128:256, 128:256].T
    cross = total[0:128, 128:256] + total[128:256, 0:128].T
    r = lax.broadcasted_iota(jnp.int32, (128, 128), 0)
    s = lax.broadcasted_iota(jnp.int32, (128, 128), 1)
    out[0:128, 0:128] = jnp.where(r <= s, first, second)
    out[0:128, 128:256] = cross
    diagonal = jnp.sum(jnp.where(r == s, second, 0.0), axis=0, keepdims=True)
    out[128:144, :] = jnp.broadcast_to(beside(diagonal, diagonal), (16, 256))


def answer_kernel(own, pa, pb, pc, gains, outputs_t, power, csd):
    packed = (own[...] + pa[...]) + (pb[...] + pc[...])
    r = lax.broadcasted_iota(jnp.int32, (128, 128), 0)
    s = lax.broadcasted_iota(jnp.int32, (128, 128), 1)
    corner = packed[0:128, 0:128]
    turned = corner.T
    diagonal = packed[128:129, 0:128]
    first = jnp.where(r <= s, corner, turned)
    second = jnp.where(r > s, corner, jnp.where(r == s, diagonal, turned))
    cross = packed[0:128, 128:256]
    whole = jnp.concatenate([beside(first, cross), beside(cross.T, second)], axis=0)
    csd[...] = whole
    g = gains[...]
    columns = jnp.transpose(g, (1, 0))
    weight = columns[:, 0:1] * g[0:1, :] + columns[:, 1:2] * g[1:2, :]
    weighted = (weight * whole).astype(jnp.bfloat16)
    width = 512
    for k in range(outputs_t.shape[1] // width):
        part = outputs_t[:, k * width : (k + 1) * width]
        mapped = dot(weighted, part)
        power[:, k * width : (k + 1) * width] = jnp.sum(mapped * part.astype(jnp.float32), axis=0, keepdims=True)


VMEM = pl.BlockSpec(memory_space=pltpu.VMEM)
SMEM = pl.BlockSpec(memory_space=pltpu.SMEM)


def call(kernel, specs, outs, *operands):
    return pl.pallas_call(
        kernel,
        in_specs=specs,
        out_specs=[VMEM] * len(outs) if len(outs) > 1 else VMEM,
        out_shape=outs if len(outs) > 1 else outs[0],
        compiler_params=pltpu.CompilerParams(vmem_limit_bytes=24 * 2**20),
    )(*operands)


def four_chips(packed, first, second, kind):
    core = lax.axis_index("col") & 1
    sent = packed.astype(kind)
    half = sent.shape[0] // 2
    far = receive(sent, lambda chip, c: (chip ^ (second if c == 0 else first ^ second), c))
    part = lax.dynamic_slice_in_dim(sent, core * half, half, 0)
    near = receive(part, lambda chip, c: (chip ^ first, c))
    far_other = other_core(far)
    near_other = other_core(near)
    near_all = jnp.where(
        core == 0,
        jnp.concatenate([near, near_other], axis=0),
        jnp.concatenate([near_other, near], axis=0),
    )
    return sent, near_all, far, far_other


def local_chips(coords, mode_shapes, output_shapes, response_gain):
    row, col = lax.axis_index("row"), lax.axis_index("col")
    core = col & 1
    x, y, z = col >> 1, row & 1, (row >> 1) & 1
    bits = jnp.stack(
        [
            core,
            jnp.where(core == 0, x, y),
            jnp.where(core == 0, 1 - y, y),
            z,
        ]
    ).astype(jnp.int32)
    blank = jnp.zeros((5, coords.shape[1]), jnp.bfloat16)
    high = (coords >> 8).astype(jnp.bfloat16)
    low = (coords & 255).astype(jnp.bfloat16)
    packed = jnp.concatenate([mode_shapes, high, blank, low, blank], axis=0)
    c_own = receive(packed, lambda chip, c: (chip ^ (BIT_W if chip < BIT_W else BIT_W | BIT_Z), c))
    own = jnp.stack([packed, other_core(packed)])
    a = receive(own, lambda chip, c: (chip ^ (BIT_X if c == 0 else BIT_Y), c))
    b = receive(own, lambda chip, c: (chip ^ (BIT_Z if c == 0 else BIT_X | BIT_Y | BIT_Z), c))
    c_other = other_core(c_own)
    e = other_core(a)
    modes = mode_shapes.shape[0]
    square = jax.ShapeDtypeStruct((modes, modes), jnp.float32)
    tri = jax.ShapeDtypeStruct((modes // 2 + 16, modes), jnp.float32)
    early = call(early_kernel, [VMEM] * 5 + [SMEM], [square], own, a, e, c_own, c_other, bits)
    mine = call(late_kernel, [VMEM] * 6 + [SMEM, VMEM], [tri], own, a, b, e, c_own, c_other, bits, early)
    chip_sum = mine + other_core(mine)
    s, pa, pb, pc = four_chips(chip_sum, BIT_Z, BIT_W, jnp.bfloat16)
    f = jnp.float32
    line_sum = (s.astype(f) + pa.astype(f)) + (pb.astype(f) + pc.astype(f))
    s, pa, pb, pc = four_chips(line_sum, BIT_X, BIT_Y, jnp.float32)
    count = output_shapes.shape[0]
    power, csd = call(
        answer_kernel,
        [VMEM] * 6,
        [jax.ShapeDtypeStruct((1, count), jnp.float32), square],
        s,
        pa,
        pb,
        pc,
        response_gain,
        output_shapes.T,
    )
    return (power.reshape(count), csd)


def solution(mesh):
    in_specs = (P(None, axes), P(None, axes), P(axes, None), P())
    out_specs = (P(axes), P())

    def whole(coords, mode_shapes, output_shapes, response_gain):
        shape = (mode_shapes.shape[0], mode_shapes.shape[1] // mesh.size)
        chips = mesh.shape["row"] == 8 and mesh.shape["col"] == 4 and shape == (256, 128)
        local = local_chips if chips else local_general
        return jax.shard_map(local, mesh=mesh, in_specs=in_specs, out_specs=out_specs, check_vma=False)(
            coords, mode_shapes, output_shapes, response_gain
        )

    return whole
```

```python
import functools
import math

import jax
import jax.numpy as jnp
from jax import lax
from jax.experimental import pallas as pl
from jax.experimental.pallas import tpu as pltpu
from jax.sharding import PartitionSpec as P

wave_scale = 0.35 / 64.0
sine_terms = (
    0.9999999970821931,
    -0.6449338560287435,
    0.1668058873098644,
    -0.023932847910373648,
    0.0021836636774330933,
    -0.00012284698513521545,
)
period_shift = 1.5 * 2.0**24
axes = ("row", "col")
POINT_ROWS = 16
BOUND_ROW = 136


def coherence(left_points, right_points):
    difference = (left_points[:, :, None] - right_points[:, None, :]).astype(jnp.float32)
    squared = jnp.sum(difference * difference, axis=0)
    return jnp.sinc(wave_scale * jnp.sqrt(squared)).astype(jnp.bfloat16)


def split_parts(matrix):
    high_part = matrix.astype(jnp.bfloat16)
    low_part = (matrix - high_part.astype(jnp.float32)).astype(jnp.bfloat16)
    return (high_part, low_part)


def modal_product(node_shapes, node_projection):
    high_part, low_part = split_parts(node_projection)
    dims = (((1,), (1,)), ((), ()))
    upper = lax.dot_general(node_shapes, high_part, dims, preferred_element_type=jnp.float32)
    lower = lax.dot_general(node_shapes, low_part, dims, preferred_element_type=jnp.float32)
    return upper + lower


def local_general(coords, mode_shapes, output_shapes, response_gain):
    row_shapes = lax.all_gather(mode_shapes, "col", axis=1, tiled=True)
    row_points = lax.all_gather(coords, "col", axis=1, tiled=True)
    mode_count = mode_shapes.shape[0]
    piece_shapes = lax.all_gather(mode_shapes, "row", axis=1, tiled=True)
    piece_points = lax.all_gather(coords, "row", axis=1, tiled=True)
    length = piece_shapes.shape[1]
    block_size = math.gcd(length, 1024)

    def add_block(loop_index, running_sum):
        block_start = loop_index * block_size
        part_shapes = lax.dynamic_slice_in_dim(piece_shapes, block_start, block_size, 1)
        part_points = lax.dynamic_slice_in_dim(piece_points, block_start, block_size, 1)
        tile = coherence(part_points, row_points)
        return running_sum + jnp.dot(part_shapes, tile, preferred_element_type=jnp.float32)

    zero_block = jnp.zeros((mode_count, row_points.shape[1]), jnp.float32)
    projection = lax.fori_loop(0, length // block_size, add_block, zero_block)
    modal_csd = lax.psum(modal_product(row_shapes, projection), axes)
    real_part, imag_part = response_gain[0], response_gain[1]
    gains = real_part[:, None] * real_part[None, :] + imag_part[:, None] * imag_part[None, :]
    weighted_high, weighted_low = split_parts(gains * modal_csd)
    mapped = jnp.dot(output_shapes, weighted_high, preferred_element_type=jnp.float32)
    mapped = mapped + jnp.dot(output_shapes, weighted_low, preferred_element_type=jnp.float32)
    response_power = jnp.sum(mapped * output_shapes.astype(jnp.float32), axis=1)
    return (response_power, modal_csd)


BIT_X, BIT_Y, BIT_Z, BIT_W = 1, 2, 4, 8


def receive(array, source):
    count = lax.axis_size(axes)
    pairs = []
    for device in range(count):
        chip, core = source(device >> 1, device & 1)
        pairs.append((chip * 2 + core, device))
    return lax.ppermute(array, axes, pairs)


def other_core(array):
    return receive(array, lambda chip, core: (chip, 1 - core))


def left_points(block):
    rows = block[256 : 256 + POINT_ROWS, :].astype(jnp.float32)
    points = rows[0:8, :] * 256.0 + rows[8:16, :]
    columns = jnp.transpose(points, (1, 0))
    return [columns[:, k : k + 1] for k in range(3)]


def right_points(block):
    rows = block[256 : 256 + POINT_ROWS, :].astype(jnp.float32)
    points = rows[0:8, :] * 256.0 + rows[8:16, :]
    return [points[k : k + 1, :] for k in range(3)]


def coherence_tile(left, right):
    squared = None
    for left_column, right_row in zip(left, right):
        difference = left_column - right_row
        term = difference * difference
        squared = term if squared is None else squared + term
    squared = jnp.maximum(squared, 1e-6)
    inverse = lax.rsqrt(squared)
    x = squared * (inverse * wave_scale)
    r = x - ((x + period_shift) - period_shift)
    z = r * r
    scale = 1.0 / wave_scale
    q = jnp.full_like(z, sine_terms[-1] * scale)
    for term in sine_terms[-2::-1]:
        q = q * z + term * scale
    return ((r * (1.0 - z)) * (q * inverse)).astype(jnp.bfloat16)


def dot(a, b):
    return jnp.dot(a, b, preferred_element_type=jnp.float32)


def dot_t(a, b):
    return lax.dot_general(a, b, (((1,), (1,)), ((), ())), preferred_element_type=jnp.float32)


def beside(*arrays):
    return jnp.concatenate(arrays, axis=1)


def shapes_of(block):
    return block[0:256, :]


def quarter(left_block, right_block):
    tile = coherence_tile(left_points(left_block), right_points(right_block))
    return dot(shapes_of(left_block), tile).astype(jnp.bfloat16), shapes_of(right_block)


def full_pair(left_halves, right_halves):
    lefts = [left_points(h) for h in left_halves]
    rights = [right_points(h) for h in right_halves]
    shapes = beside(*[shapes_of(h) for h in left_halves])
    projections = []
    for right in rights:
        column = jnp.concatenate([coherence_tile(left, right) for left in lefts], axis=0)
        projections.append(dot(shapes, column).astype(jnp.bfloat16))
    return dot_t(beside(*projections), beside(*[shapes_of(h) for h in right_halves]))


def paired(jobs):
    projections, shapes = zip(*jobs)
    return dot_t(beside(*projections), beside(*shapes))


def place():
    row, col = lax.axis_index("row"), lax.axis_index("col")
    return col & 1, col >> 1, row & 1, (row >> 1) & 1


def early_kernel(own, a, e, c_own, c_other, response_gain, out, gains):
    gains[...] = response_gain[...]
    core, x, y, _ = place()
    mine = right_points(own[0])
    total = 0.5 * dot_t(
        dot(
            beside(shapes_of(own[0]), shapes_of(own[1])),
            jnp.concatenate(
                [coherence_tile(left_points(own[0]), mine), coherence_tile(left_points(own[1]), mine)], axis=0
            ),
        ).astype(jnp.bfloat16),
        shapes_of(own[0]),
    )
    u = jnp.where(core == 0, x, y)
    jobs = []
    for k in range(2):
        left_half, right_half = u * k, u | k
        jobs.append(quarter(own[left_half ^ core], a[right_half ^ core]))
    total += paired(jobs)
    u = jnp.where(core == 0, 1 - y, y)
    left_half = jnp.where(u == 1, 1, core)
    right_half = jnp.where(u == 1, core, 0)
    projection, shapes = quarter(e[left_half ^ (1 - core)], a[right_half ^ core])
    total += dot_t(projection, shapes)
    total += full_pair([a[0], a[1]], [c_own[...], c_other[...]])
    out[...] = total


def late_kernel(own, a, b, e, c_own, c_other, early, out):
    core, _, _, u = place()
    total = early[...]
    jobs = []
    for k in range(2):
        left_half, right_half = u * k, u | k
        jobs.append(quarter(own[left_half ^ core], b[right_half ^ core]))
    total += paired(jobs)
    left_half = jnp.where(u == 1, 1, core)
    right_half = jnp.where(u == 1, core, 0)
    right = b[right_half ^ core]
    total += paired([quarter(a[left_half ^ core], right), quarter(e[left_half ^ (1 - core)], right)])
    total += full_pair([b[0], b[1]], [c_own[...], c_other[...]])
    first = total[0:128, 0:128] + total[0:128, 0:128].T
    second = total[128:256, 128:256] + total[128:256, 128:256].T
    cross = total[0:128, 128:256] + total[128:256, 0:128].T
    r = lax.broadcasted_iota(jnp.int32, (128, 128), 0)
    s = lax.broadcasted_iota(jnp.int32, (128, 128), 1)
    out[0:128, 0:128] = jnp.where(r <= s, first, second)
    out[0:128, 128:256] = cross
    diagonal = jnp.sum(jnp.where(r == s, second, 0.0), axis=0, keepdims=True)
    out[128:BOUND_ROW, :] = jnp.broadcast_to(beside(diagonal, diagonal), (8, 256))
    largest = jnp.maximum(jnp.abs(out[0:128, :]), jnp.abs(out[128:129, :]))
    largest = jnp.max(jnp.max(largest, axis=0, keepdims=True), axis=1, keepdims=True)
    out[BOUND_ROW:, :] = jnp.broadcast_to(largest, (8, 256))


def answer_kernel(total, gains, outputs_t, power, csd):
    packed = total[...]
    r = lax.broadcasted_iota(jnp.int32, (128, 128), 0)
    s = lax.broadcasted_iota(jnp.int32, (128, 128), 1)
    corner = packed[0:128, 0:128]
    turned = corner.T
    diagonal = packed[128:129, 0:128]
    first = jnp.where(r <= s, corner, turned)
    second = jnp.where(r > s, corner, jnp.where(r == s, diagonal, turned))
    cross = packed[0:128, 128:256]
    whole = jnp.concatenate([beside(first, cross), beside(cross.T, second)], axis=0)
    csd[...] = whole
    g = gains[...]
    columns = jnp.transpose(g, (1, 0))
    weight = columns[:, 0:1] * g[0:1, :] + columns[:, 1:2] * g[1:2, :]
    weighted = (weight * whole).astype(jnp.bfloat16)
    width = 512
    for k in range(outputs_t.shape[1] // width):
        part = outputs_t[:, k * width : (k + 1) * width]
        mapped = dot(weighted, part)
        power[:, k * width : (k + 1) * width] = jnp.sum(mapped * part.astype(jnp.float32), axis=0, keepdims=True)


VMEM = pl.BlockSpec(memory_space=pltpu.VMEM)


def call(kernel, specs, outs, *operands, cost=None):
    return pl.pallas_call(
        kernel,
        in_specs=specs,
        out_specs=[VMEM] * len(outs) if len(outs) > 1 else VMEM,
        out_shape=outs if len(outs) > 1 else outs[0],
        cost_estimate=cost and pl.CostEstimate(flops=cost, bytes_accessed=0, transcendentals=0),
        compiler_params=pltpu.CompilerParams(vmem_limit_bytes=24 * 2**20),
    )(*operands)


def four_chips(sent, first, second):
    core = lax.axis_index("col") & 1
    half = sent.shape[0] // 2
    far = receive(sent, lambda chip, c: (chip ^ (second if c == 0 else first ^ second), c))
    part = lax.dynamic_slice_in_dim(sent, core * half, half, 0)
    near = receive(part, lambda chip, c: (chip ^ first, c))
    far_other = other_core(far)
    near_other = other_core(near)
    near_all = jnp.where(
        core == 0,
        jnp.concatenate([near, near_other], axis=0),
        jnp.concatenate([near_other, near], axis=0),
    )
    return near_all, far, far_other


def scaled(packed):
    exponent = jnp.clip(jnp.round(jnp.log2(packed[BOUND_ROW : BOUND_ROW + 1])), -100.0, 100.0)
    row = lax.broadcasted_iota(jnp.int32, packed.shape, 0)
    return jnp.where(row < BOUND_ROW, packed * jnp.exp2(-exponent), exponent).astype(jnp.float16)


def unscaled(sent):
    wide = sent.astype(jnp.float32)
    return wide * jnp.exp2(wide[BOUND_ROW : BOUND_ROW + 1])


def pack(mode_shapes, coords):
    modes = mode_shapes.shape[0]
    high, low = (coords >> 8).astype(jnp.bfloat16), (coords & 255).astype(jnp.bfloat16)
    return (
        jnp.pad(mode_shapes, ((0, POINT_ROWS), (0, 0)))
        + jnp.pad(high, ((modes, POINT_ROWS - 3), (0, 0)))
        + jnp.pad(low, ((modes + 8, POINT_ROWS - 11), (0, 0)))
    )


def local_chips(coords, mode_shapes, output_shapes, response_gain):
    modes, nodes = mode_shapes.shape
    packed = pack(mode_shapes, coords)
    own = jnp.stack([packed, pack(other_core(mode_shapes), other_core(coords))])
    c_own = receive(packed, lambda chip, c: (chip ^ (BIT_W if chip < BIT_W else BIT_W | BIT_Z), c))
    a = receive(own, lambda chip, c: (chip ^ (BIT_X if c == 0 else BIT_Y), c))
    b = receive(own, lambda chip, c: (chip ^ (BIT_Z if c == 0 else BIT_X | BIT_Y | BIT_Z), c))
    c_other = other_core(c_own)
    e = other_core(a)
    square = jax.ShapeDtypeStruct((modes, modes), jnp.float32)
    tri = jax.ShapeDtypeStruct((modes // 2 + 16, modes), jnp.float32)
    gain_rows = jax.ShapeDtypeStruct(response_gain.shape, jnp.float32)
    early, gains = call(early_kernel, [VMEM] * 6, [square, gain_rows], own, a, e, c_own, c_other, response_gain)
    mine = call(late_kernel, [VMEM] * 7, [tri], own, a, b, e, c_own, c_other, early)
    chip_sum = mine + other_core(mine)
    f = jnp.float32
    sent = chip_sum.astype(jnp.bfloat16)
    pa, pb, pc = four_chips(sent, BIT_Z, BIT_W)
    line_sum = (sent.astype(f) + pa.astype(f)) + (pb.astype(f) + pc.astype(f))
    sent = scaled(line_sum)
    pa, pb, pc = four_chips(sent, BIT_X, BIT_Y)
    total = (unscaled(sent) + unscaled(pa)) + (unscaled(pb) + unscaled(pc))
    count = output_shapes.shape[0]
    power, csd = call(
        answer_kernel,
        [VMEM] * 3,
        [jax.ShapeDtypeStruct((1, count), jnp.float32), square],
        total,
        gains,
        output_shapes.T,
    )
    return (power.reshape(count), csd)


def solution(mesh):
    in_specs = (P(None, axes), P(None, axes), P(axes, None), P())
    out_specs = (P(axes), P())

    def whole(coords, mode_shapes, output_shapes, response_gain):
        shape = (mode_shapes.shape[0], mode_shapes.shape[1] // mesh.size)
        chips = mesh.shape["row"] == 8 and mesh.shape["col"] == 4 and shape == (256, 128)
        local = local_chips if chips else local_general
        return jax.shard_map(local, mesh=mesh, in_specs=in_specs, out_specs=out_specs, check_vma=False)(
            coords, mode_shapes, output_shapes, response_gain
        )

    return whole
```

```python
import math

import jax
import jax.numpy as jnp
from jax import lax
from jax.experimental import pallas as pl
from jax.experimental.pallas import tpu as pltpu
from jax.sharding import PartitionSpec as P

wave_scale = 0.35 / 64.0
sine_terms = (
    0.9999999970821931,
    -0.6449338560287435,
    0.1668058873098644,
    -0.023932847910373648,
    0.0021836636774330933,
    -0.00012284698513521545,
)
period_shift = 1.5 * 2.0**24
axes = ("row", "col")
POINT_ROWS = 16
BOUND_ROW = 132


def coherence(left_points, right_points):
    difference = (left_points[:, :, None] - right_points[:, None, :]).astype(jnp.float32)
    squared = jnp.sum(difference * difference, axis=0)
    return jnp.sinc(wave_scale * jnp.sqrt(squared)).astype(jnp.bfloat16)


def split_parts(matrix):
    high_part = matrix.astype(jnp.bfloat16)
    low_part = (matrix - high_part.astype(jnp.float32)).astype(jnp.bfloat16)
    return (high_part, low_part)


def modal_product(node_shapes, node_projection):
    high_part, low_part = split_parts(node_projection)
    dims = (((1,), (1,)), ((), ()))
    upper = lax.dot_general(node_shapes, high_part, dims, preferred_element_type=jnp.float32)
    lower = lax.dot_general(node_shapes, low_part, dims, preferred_element_type=jnp.float32)
    return upper + lower


def local_general(coords, mode_shapes, output_shapes, response_gain):
    row_shapes = lax.all_gather(mode_shapes, "col", axis=1, tiled=True)
    row_points = lax.all_gather(coords, "col", axis=1, tiled=True)
    mode_count = mode_shapes.shape[0]
    piece_shapes = lax.all_gather(mode_shapes, "row", axis=1, tiled=True)
    piece_points = lax.all_gather(coords, "row", axis=1, tiled=True)
    length = piece_shapes.shape[1]
    block_size = math.gcd(length, 1024)

    def add_block(loop_index, running_sum):
        block_start = loop_index * block_size
        part_shapes = lax.dynamic_slice_in_dim(piece_shapes, block_start, block_size, 1)
        part_points = lax.dynamic_slice_in_dim(piece_points, block_start, block_size, 1)
        tile = coherence(part_points, row_points)
        return running_sum + jnp.dot(part_shapes, tile, preferred_element_type=jnp.float32)

    zero_block = jnp.zeros((mode_count, row_points.shape[1]), jnp.float32)
    projection = lax.fori_loop(0, length // block_size, add_block, zero_block)
    modal_csd = lax.psum(modal_product(row_shapes, projection), axes)
    real_part, imag_part = response_gain[0], response_gain[1]
    gains = real_part[:, None] * real_part[None, :] + imag_part[:, None] * imag_part[None, :]
    weighted_high, weighted_low = split_parts(gains * modal_csd)
    mapped = jnp.dot(output_shapes, weighted_high, preferred_element_type=jnp.float32)
    mapped = mapped + jnp.dot(output_shapes, weighted_low, preferred_element_type=jnp.float32)
    response_power = jnp.sum(mapped * output_shapes.astype(jnp.float32), axis=1)
    return (response_power, modal_csd)


BIT_X, BIT_Y, BIT_Z, BIT_W = 1, 2, 4, 8
OFFSET_A = (4, 6)
OFFSET_B = (1, 3)
OFFSET_C = (8, 12)


def receive(array, source):
    count = lax.axis_size(axes)
    pairs = []
    for device in range(count):
        chip, core = source(device >> 1, device & 1)
        pairs.append((chip * 2 + core, device))
    return lax.ppermute(array, axes, pairs)


def other_core(array):
    return receive(array, lambda chip, core: (chip, 1 - core))


def left_points(block):
    rows = block[256 : 256 + POINT_ROWS, :].astype(jnp.float32)
    points = rows[0:8, :] * 256.0 + rows[8:16, :]
    columns = jnp.transpose(points, (1, 0))
    return [columns[:, k : k + 1] for k in range(3)]


def right_points(block):
    rows = block[256 : 256 + POINT_ROWS, :].astype(jnp.float32)
    points = rows[0:8, :] * 256.0 + rows[8:16, :]
    return [points[k : k + 1, :] for k in range(3)]


def coherence_tile(left, right):
    squared = None
    for left_column, right_row in zip(left, right):
        difference = left_column - right_row
        term = difference * difference
        squared = term if squared is None else squared + term
    squared = jnp.maximum(squared, 1e-6)
    inverse = lax.rsqrt(squared)
    x = squared * (inverse * wave_scale)
    r = x - ((x + period_shift) - period_shift)
    z = r * r
    scale = 1.0 / wave_scale
    q = jnp.full_like(z, sine_terms[-1] * scale)
    for term in sine_terms[-2::-1]:
        q = q * z + term * scale
    return ((r * (1.0 - z)) * (q * inverse)).astype(jnp.bfloat16)


def dot(a, b):
    return jnp.dot(a, b, preferred_element_type=jnp.float32)


def dot_t(a, b):
    return lax.dot_general(a, b, (((1,), (1,)), ((), ())), preferred_element_type=jnp.float32)


def beside(*arrays):
    return jnp.concatenate(arrays, axis=1)


def shapes_of(block):
    return block[0:256, :]


def quarter(left_block, right_block):
    tile = coherence_tile(left_points(left_block), right_points(right_block))
    return dot(shapes_of(left_block), tile).astype(jnp.bfloat16), shapes_of(right_block)


def full_pair(left_halves, right_halves):
    lefts = [left_points(h) for h in left_halves]
    rights = [right_points(h) for h in right_halves]
    shapes = beside(*[shapes_of(h) for h in left_halves])
    projections = []
    for right in rights:
        column = jnp.concatenate([coherence_tile(left, right) for left in lefts], axis=0)
        projections.append(dot(shapes, column).astype(jnp.bfloat16))
    return dot_t(beside(*projections), beside(*[shapes_of(h) for h in right_halves]))


def paired(jobs):
    projections, shapes = zip(*jobs)
    return dot_t(beside(*projections), beside(*shapes))


def upper_bits(*roles):
    row, col = lax.axis_index("row"), lax.axis_index("col")
    core, chip = col & 1, row * 2 + (col >> 1)
    found = []
    for left_0, left_1, right_0, right_1 in roles:
        shift_0, shift_1 = ((d & -d).bit_length() - 1 for d in (left_0 ^ right_0, left_1 ^ right_1))
        on_0, on_1 = ((chip ^ left_0) >> shift_0) & 1, ((chip ^ left_1) >> shift_1) & 1
        found.append(jnp.where(core == 0, on_0, on_1))
    return found


ROLE_S, ROLE_A, ROLE_B, ROLE_E = (0, 0), OFFSET_A, OFFSET_B, OFFSET_A[::-1]


def early_kernel(own, a, e, c_own, c_other, response_gain, out, gains):
    gains[...] = response_gain[...]
    sa, ea = upper_bits(ROLE_S + ROLE_A, ROLE_E + ROLE_A)
    total = paired([quarter(own[0], a[1]), quarter(own[sa], a[sa]), quarter(e[...], a[ea])])
    total += full_pair([a[0], a[1]], [c_own[...], c_other[...]])
    total += 0.5 * full_pair([own[0], own[1]], [own[0]])
    out[...] = total


def late_kernel(own, a, b, e, c_own, c_other, early, out):
    sb, ab, eb = upper_bits(ROLE_S + ROLE_B, ROLE_A + ROLE_B, ROLE_E + ROLE_B)
    total = early[...]
    total += full_pair([b[0], b[1]], [c_own[...], c_other[...]])
    total += paired([quarter(own[0], b[1]), quarter(own[sb], b[sb]), quarter(a[0], b[ab]), quarter(e[...], b[eb])])
    first = total[0:128, 0:128] + total[0:128, 0:128].T
    second = total[128:256, 128:256] + total[128:256, 128:256].T
    cross = total[0:128, 128:256] + total[128:256, 0:128].T
    r = lax.broadcasted_iota(jnp.int32, (128, 128), 0)
    s = lax.broadcasted_iota(jnp.int32, (128, 128), 1)
    corner = jnp.where(r <= s, first, second)
    out[0:128, 0:128] = corner
    out[0:128, 128:256] = cross
    diagonal = jnp.sum(jnp.where(r == s, second, 0.0), axis=0, keepdims=True)
    out[128:BOUND_ROW, :] = jnp.broadcast_to(beside(diagonal, diagonal), (4, 256))
    largest = jnp.maximum(jnp.max(jnp.abs(beside(corner, cross)), axis=0, keepdims=True), jnp.abs(beside(diagonal, diagonal)))
    out[BOUND_ROW:, :] = jnp.broadcast_to(largest, (out.shape[0] - BOUND_ROW, 256))


def answer_kernel(total, gains, outputs_t, power, csd):
    packed = total[...]
    r = lax.broadcasted_iota(jnp.int32, (128, 128), 0)
    s = lax.broadcasted_iota(jnp.int32, (128, 128), 1)
    corner = packed[0:128, 0:128]
    turned = corner.T
    diagonal = packed[128:129, 0:128]
    first = jnp.where(r <= s, corner, turned)
    second = jnp.where(r > s, corner, jnp.where(r == s, diagonal, turned))
    cross = packed[0:128, 128:256]
    whole = jnp.concatenate([beside(first, cross), beside(cross.T, second)], axis=0)
    csd[...] = whole
    g = gains[...]
    columns = jnp.transpose(g, (1, 0))
    weight = columns[:, 0:1] * g[0:1, :] + columns[:, 1:2] * g[1:2, :]
    weighted = (weight * whole).astype(jnp.bfloat16)
    width = 512
    for k in range(outputs_t.shape[1] // width):
        part = outputs_t[:, k * width : (k + 1) * width]
        mapped = dot(weighted, part)
        power[:, k * width : (k + 1) * width] = jnp.sum(mapped * part.astype(jnp.float32), axis=0, keepdims=True)


VMEM = pl.BlockSpec(memory_space=pltpu.VMEM)


def call(kernel, specs, outs, *operands):
    return pl.pallas_call(
        kernel,
        in_specs=specs,
        out_specs=[VMEM] * len(outs) if len(outs) > 1 else VMEM,
        out_shape=outs if len(outs) > 1 else outs[0],
        compiler_params=pltpu.CompilerParams(vmem_limit_bytes=24 * 2**20),
    )(*operands)


def four_chips(sent, first, second):
    core = lax.axis_index("col") & 1
    half = 72
    rest = sent.shape[0] - half
    far = receive(sent, lambda chip, c: (chip ^ (second if c == 0 else first ^ second), c))
    part = lax.dynamic_slice_in_dim(sent, core * rest, half, 0)
    near = receive(part, lambda chip, c: (chip ^ first, c))
    far_other = other_core(far)
    near_other = other_core(near)
    near_all = jnp.where(
        core == 0,
        jnp.concatenate([near[:rest], near_other], axis=0),
        jnp.concatenate([near_other[:rest], near], axis=0),
    )
    return near_all, far, far_other


def scaled(packed):
    exponent = jnp.clip(jnp.round(jnp.log2(packed[BOUND_ROW : BOUND_ROW + 1])), -100.0, 100.0)
    row = lax.broadcasted_iota(jnp.int32, packed.shape, 0)
    return jnp.where(row < BOUND_ROW, packed * jnp.exp2(-exponent), exponent).astype(jnp.float16)


def unscaled(sent):
    wide = sent.astype(jnp.float32)
    return wide * jnp.exp2(wide[BOUND_ROW : BOUND_ROW + 1])


def pack(mode_shapes, coords):
    modes = mode_shapes.shape[0]
    high, low = (coords >> 8).astype(jnp.bfloat16), (coords & 255).astype(jnp.bfloat16)
    return (
        jnp.pad(mode_shapes, ((0, POINT_ROWS), (0, 0)))
        + jnp.pad(high, ((modes, POINT_ROWS - 3), (0, 0)))
        + jnp.pad(low, ((modes + 8, POINT_ROWS - 11), (0, 0)))
    )


def local_chips(coords, mode_shapes, output_shapes, response_gain):
    modes, nodes = mode_shapes.shape
    packed = pack(mode_shapes, coords)
    own = jnp.stack([packed, pack(other_core(mode_shapes), other_core(coords))])
    c_own = receive(packed, lambda chip, c: (chip ^ OFFSET_C[0 if chip < BIT_W else 1], c))
    a = receive(own, lambda chip, c: (chip ^ OFFSET_A[c], c))
    b = receive(own, lambda chip, c: (chip ^ OFFSET_B[c], c))
    c_other = other_core(c_own)
    e = other_core(a[1])
    square = jax.ShapeDtypeStruct((modes, modes), jnp.float32)
    tri = jax.ShapeDtypeStruct((modes // 2 + 8, modes), jnp.float32)
    gain_rows = jax.ShapeDtypeStruct(response_gain.shape, jnp.float32)
    early, gains = call(early_kernel, [VMEM] * 6, [square, gain_rows], own, a, e, c_own, c_other, response_gain)
    mine = call(late_kernel, [VMEM] * 7, [tri], own, a, b, e, c_own, c_other, early)
    chip_sum = mine + other_core(mine)
    f = jnp.float32
    sent = chip_sum.astype(jnp.bfloat16)
    pa, pb, pc = four_chips(sent, BIT_Z, BIT_W)
    line_sum = (sent.astype(f) + pa.astype(f)) + (pb.astype(f) + pc.astype(f))
    sent = scaled(line_sum)
    pa, pb, pc = four_chips(sent, BIT_X, BIT_Y)
    total = (unscaled(sent) + unscaled(pa)) + (unscaled(pb) + unscaled(pc))
    count = output_shapes.shape[0]
    power, csd = call(
        answer_kernel,
        [VMEM] * 3,
        [jax.ShapeDtypeStruct((1, count), jnp.float32), square],
        total,
        gains,
        output_shapes.T,
    )
    return (power.reshape(count), csd)


def solution(mesh):
    in_specs = (P(None, axes), P(None, axes), P(axes, None), P())
    out_specs = (P(axes), P())

    def whole(coords, mode_shapes, output_shapes, response_gain):
        shape = (mode_shapes.shape[0], mode_shapes.shape[1] // mesh.size)
        chips = mesh.shape["row"] == 8 and mesh.shape["col"] == 4 and shape == (256, 128)
        local = local_chips if chips else local_general
        return jax.shard_map(local, mesh=mesh, in_specs=in_specs, out_specs=out_specs, check_vma=False)(
            coords, mode_shapes, output_shapes, response_gain
        )

    return whole
```

```python
import math

import jax
import jax.numpy as jnp
from jax import lax
from jax.experimental import pallas as pl
from jax.experimental.pallas import tpu as pltpu
from jax.sharding import PartitionSpec as P

wave_scale = 0.35 / 64.0
sine_terms = (
    0.9999999970821931,
    -0.6449338560287435,
    0.1668058873098644,
    -0.023932847910373648,
    0.0021836636774330933,
    -0.00012284698513521545,
)
period_shift = 1.5 * 2.0**24
axes = ("row", "col")
POINT_ROWS = 16
BOUND_ROW = 132


def coherence(left_points, right_points):
    difference = (left_points[:, :, None] - right_points[:, None, :]).astype(jnp.float32)
    squared = jnp.sum(difference * difference, axis=0)
    return jnp.sinc(wave_scale * jnp.sqrt(squared)).astype(jnp.bfloat16)


def split_parts(matrix):
    high_part = matrix.astype(jnp.bfloat16)
    low_part = (matrix - high_part.astype(jnp.float32)).astype(jnp.bfloat16)
    return (high_part, low_part)


def modal_product(node_shapes, node_projection):
    high_part, low_part = split_parts(node_projection)
    dims = (((1,), (1,)), ((), ()))
    upper = lax.dot_general(node_shapes, high_part, dims, preferred_element_type=jnp.float32)
    lower = lax.dot_general(node_shapes, low_part, dims, preferred_element_type=jnp.float32)
    return upper + lower


def local_general(coords, mode_shapes, output_shapes, response_gain):
    row_shapes = lax.all_gather(mode_shapes, "col", axis=1, tiled=True)
    row_points = lax.all_gather(coords, "col", axis=1, tiled=True)
    mode_count = mode_shapes.shape[0]
    piece_shapes = lax.all_gather(mode_shapes, "row", axis=1, tiled=True)
    piece_points = lax.all_gather(coords, "row", axis=1, tiled=True)
    length = piece_shapes.shape[1]
    block_size = math.gcd(length, 1024)

    def add_block(loop_index, running_sum):
        block_start = loop_index * block_size
        part_shapes = lax.dynamic_slice_in_dim(piece_shapes, block_start, block_size, 1)
        part_points = lax.dynamic_slice_in_dim(piece_points, block_start, block_size, 1)
        tile = coherence(part_points, row_points)
        return running_sum + jnp.dot(part_shapes, tile, preferred_element_type=jnp.float32)

    zero_block = jnp.zeros((mode_count, row_points.shape[1]), jnp.float32)
    projection = lax.fori_loop(0, length // block_size, add_block, zero_block)
    modal_csd = lax.psum(modal_product(row_shapes, projection), axes)
    real_part, imag_part = response_gain[0], response_gain[1]
    gains = real_part[:, None] * real_part[None, :] + imag_part[:, None] * imag_part[None, :]
    weighted_high, weighted_low = split_parts(gains * modal_csd)
    mapped = jnp.dot(output_shapes, weighted_high, preferred_element_type=jnp.float32)
    mapped = mapped + jnp.dot(output_shapes, weighted_low, preferred_element_type=jnp.float32)
    response_power = jnp.sum(mapped * output_shapes.astype(jnp.float32), axis=1)
    return (response_power, modal_csd)


BIT_X, BIT_Y, BIT_Z, BIT_W = 1, 2, 4, 8
CHIP_AT = (2, 0, 14, 12, 4, 6, 9, 8, 3, 1, 15, 13, 5, 7, 11, 10)
OFFSET_A = ((0, 1), (1, 0))
OFFSET_B = ((4, 0), (6, 1))


def moved(place, offset):
    return (place[0] + offset[0]) % 8, (place[1] + offset[1]) % 2


def partner(chip, offset):
    place = CHIP_AT.index(chip)
    i, j = moved((place // 2, place % 2), offset)
    return CHIP_AT[2 * i + j]


def share(left, right):
    shares = []
    for l, r in zip(left, right):
        difference = (r[0] - l[0]) % 8, (r[1] - l[1]) % 2
        shares.append(0.5 if moved(difference, difference) == (0, 0) else 1.0)
    return tuple(shares)


ROLE_S = ((0, 0), (0, 0))
assert share(ROLE_S, OFFSET_A) == share(ROLE_S, OFFSET_B) == share(OFFSET_A, OFFSET_B)
assert share(OFFSET_A, OFFSET_A[::-1]) == share(OFFSET_A[::-1], OFFSET_B) == (1.0, 1.0)


def receive(array, source):
    count = lax.axis_size(axes)
    pairs = []
    for device in range(count):
        chip, core = source(device >> 1, device & 1)
        pairs.append((chip * 2 + core, device))
    return lax.ppermute(array, axes, pairs)


def other_core(array):
    return receive(array, lambda chip, core: (chip, 1 - core))


def left_points(block):
    rows = block[256 : 256 + POINT_ROWS, :].astype(jnp.float32)
    points = rows[0:8, :] * 256.0 + rows[8:16, :]
    columns = jnp.transpose(points, (1, 0))
    return [columns[:, k : k + 1] for k in range(3)]


def right_points(block):
    rows = block[256 : 256 + POINT_ROWS, :].astype(jnp.float32)
    points = rows[0:8, :] * 256.0 + rows[8:16, :]
    return [points[k : k + 1, :] for k in range(3)]


def coherence_tile(left, right):
    squared = None
    for left_column, right_row in zip(left, right):
        difference = left_column - right_row
        term = difference * difference
        squared = term if squared is None else squared + term
    squared = jnp.maximum(squared, 1e-6)
    inverse = lax.rsqrt(squared)
    x = squared * (inverse * wave_scale)
    r = x - ((x + period_shift) - period_shift)
    z = r * r
    scale = 1.0 / wave_scale
    q = jnp.full_like(z, sine_terms[-1] * scale)
    for term in sine_terms[-2::-1]:
        q = q * z + term * scale
    return ((r * (1.0 - z)) * (q * inverse)).astype(jnp.bfloat16)


def dot(a, b):
    return jnp.dot(a, b, preferred_element_type=jnp.float32)


def dot_t(a, b):
    return lax.dot_general(a, b, (((1,), (1,)), ((), ())), preferred_element_type=jnp.float32)


def beside(*arrays):
    return jnp.concatenate(arrays, axis=1)


def shapes_of(block):
    return block[0:256, :]


def projection(left_halves, right_half):
    right = right_points(right_half)
    tiles = [coherence_tile(left_points(half), right) for half in left_halves]
    return dot(beside(*[shapes_of(half) for half in left_halves]), jnp.concatenate(tiles, axis=0))


def modal(projections, right_halves):
    return dot_t(
        beside(*[p.astype(jnp.bfloat16) for p in projections]), beside(*[shapes_of(half) for half in right_halves])
    )


def this_core():
    return lax.axis_index("col") & 1


def own_share():
    on_0, on_1 = share(ROLE_S, OFFSET_A)
    return jnp.where(this_core() == 0, on_0, on_1).astype(jnp.float32)


def early_kernel(own, a, response_gain, out, gains):
    gains[...] = response_gain[...]
    weight = own_share()
    pairs = [weight * projection([own[0], own[1]], a[k]) for k in range(2)]
    pairs.append(0.5 * projection([own[0], own[1]], own[0]))
    out[...] = modal(pairs, [a[0], a[1], own[0]])


def late_kernel(own, a, b, e0, e1, early, out):
    weight = own_share()
    pairs = [
        weight * projection([own[0], own[1], a[0], a[1]], b[k]) + projection([e0[...], e1[...]], b[k]) for k in range(2)
    ]
    core = this_core()
    pairs += [projection([a[core]], e0[...]), projection([a[1 - core]], e1[...])]
    total = early[...] + modal(pairs, [b[0], b[1], e0[...], e1[...]])
    first = total[0:128, 0:128] + total[0:128, 0:128].T
    second = total[128:256, 128:256] + total[128:256, 128:256].T
    cross = total[0:128, 128:256] + total[128:256, 0:128].T
    r = lax.broadcasted_iota(jnp.int32, (128, 128), 0)
    s = lax.broadcasted_iota(jnp.int32, (128, 128), 1)
    corner = jnp.where(r <= s, first, second)
    out[0:128, 0:128] = corner
    out[0:128, 128:256] = cross
    diagonal = jnp.sum(jnp.where(r == s, second, 0.0), axis=0, keepdims=True)
    out[128:BOUND_ROW, :] = jnp.broadcast_to(beside(diagonal, diagonal), (4, 256))
    largest = jnp.maximum(jnp.max(jnp.abs(beside(corner, cross)), axis=0, keepdims=True), jnp.abs(beside(diagonal, diagonal)))
    out[BOUND_ROW:, :] = jnp.broadcast_to(largest, (out.shape[0] - BOUND_ROW, 256))


def answer_kernel(total, gains, outputs_t, power, csd):
    packed = total[...]
    r = lax.broadcasted_iota(jnp.int32, (128, 128), 0)
    s = lax.broadcasted_iota(jnp.int32, (128, 128), 1)
    corner = packed[0:128, 0:128]
    turned = corner.T
    diagonal = packed[128:129, 0:128]
    first = jnp.where(r <= s, corner, turned)
    second = jnp.where(r > s, corner, jnp.where(r == s, diagonal, turned))
    cross = packed[0:128, 128:256]
    whole = jnp.concatenate([beside(first, cross), beside(cross.T, second)], axis=0)
    csd[...] = whole
    g = gains[...]
    columns = jnp.transpose(g, (1, 0))
    weight = columns[:, 0:1] * g[0:1, :] + columns[:, 1:2] * g[1:2, :]
    weighted = (weight * whole).astype(jnp.bfloat16)
    width = 512
    for k in range(outputs_t.shape[1] // width):
        part = outputs_t[:, k * width : (k + 1) * width]
        mapped = dot(weighted, part)
        power[:, k * width : (k + 1) * width] = jnp.sum(mapped * part.astype(jnp.float32), axis=0, keepdims=True)


VMEM = pl.BlockSpec(memory_space=pltpu.VMEM)


def call(kernel, specs, outs, *operands):
    return pl.pallas_call(
        kernel,
        in_specs=specs,
        out_specs=[VMEM] * len(outs) if len(outs) > 1 else VMEM,
        out_shape=outs if len(outs) > 1 else outs[0],
        compiler_params=pltpu.CompilerParams(vmem_limit_bytes=24 * 2**20),
    )(*operands)


def four_chips(sent, first, second):
    core = lax.axis_index("col") & 1
    half = 72
    rest = sent.shape[0] - half
    far = receive(sent, lambda chip, c: (chip ^ (second if c == 0 else first ^ second), c))
    part = lax.dynamic_slice_in_dim(sent, core * rest, half, 0)
    near = receive(part, lambda chip, c: (chip ^ first, c))
    far_other = other_core(far)
    near_other = other_core(near)
    near_all = jnp.where(
        core == 0,
        jnp.concatenate([near[:rest], near_other], axis=0),
        jnp.concatenate([near_other[:rest], near], axis=0),
    )
    return near_all, far, far_other


def scaled(packed):
    exponent = jnp.clip(jnp.round(jnp.log2(packed[BOUND_ROW : BOUND_ROW + 1])), -100.0, 100.0)
    row = lax.broadcasted_iota(jnp.int32, packed.shape, 0)
    return jnp.where(row < BOUND_ROW, packed * jnp.exp2(-exponent), exponent).astype(jnp.float16)


def unscaled(sent):
    wide = sent.astype(jnp.float32)
    return wide * jnp.exp2(wide[BOUND_ROW : BOUND_ROW + 1])


def pack(mode_shapes, coords):
    modes = mode_shapes.shape[0]
    high, low = (coords >> 8).astype(jnp.bfloat16), (coords & 255).astype(jnp.bfloat16)
    return (
        jnp.pad(mode_shapes, ((0, POINT_ROWS), (0, 0)))
        + jnp.pad(high, ((modes, POINT_ROWS - 3), (0, 0)))
        + jnp.pad(low, ((modes + 8, POINT_ROWS - 11), (0, 0)))
    )


def local_chips(coords, mode_shapes, output_shapes, response_gain):
    modes, nodes = mode_shapes.shape
    packed = pack(mode_shapes, coords)
    own = jnp.stack([packed, pack(other_core(mode_shapes), other_core(coords))])
    a = receive(own, lambda chip, c: (partner(chip, OFFSET_A[c]), c))
    b = receive(own, lambda chip, c: (partner(chip, OFFSET_B[c]), c))
    e0, e1 = other_core(a[0]), other_core(a[1])
    square = jax.ShapeDtypeStruct((modes, modes), jnp.float32)
    tri = jax.ShapeDtypeStruct((modes // 2 + 8, modes), jnp.float32)
    gain_rows = jax.ShapeDtypeStruct(response_gain.shape, jnp.float32)
    early, gains = call(early_kernel, [VMEM] * 3, [square, gain_rows], own, a, response_gain)
    mine = call(late_kernel, [VMEM] * 6, [tri], own, a, b, e0, e1, early)
    chip_sum = mine + other_core(mine)
    f = jnp.float32
    sent = chip_sum.astype(jnp.bfloat16)
    pa, pb, pc = four_chips(sent, BIT_Z, BIT_W)
    line_sum = (sent.astype(f) + pa.astype(f)) + (pb.astype(f) + pc.astype(f))
    sent = scaled(line_sum)
    pa, pb, pc = four_chips(sent, BIT_X, BIT_Y)
    total = (unscaled(sent) + unscaled(pa)) + (unscaled(pb) + unscaled(pc))
    count = output_shapes.shape[0]
    power, csd = call(
        answer_kernel,
        [VMEM] * 3,
        [jax.ShapeDtypeStruct((1, count), jnp.float32), square],
        total,
        gains,
        output_shapes.T,
    )
    return (power.reshape(count), csd)


def solution(mesh):
    in_specs = (P(None, axes), P(None, axes), P(axes, None), P())
    out_specs = (P(axes), P())

    def whole(coords, mode_shapes, output_shapes, response_gain):
        shape = (mode_shapes.shape[0], mode_shapes.shape[1] // mesh.size)
        chips = mesh.shape["row"] == 8 and mesh.shape["col"] == 4 and shape == (256, 128)
        local = local_chips if chips else local_general
        return jax.shard_map(local, mesh=mesh, in_specs=in_specs, out_specs=out_specs, check_vma=False)(
            coords, mode_shapes, output_shapes, response_gain
        )

    return whole
```

```python
import math

import jax
import jax.numpy as jnp
from jax import lax
from jax.experimental import pallas as pl
from jax.experimental.pallas import tpu as pltpu
from jax.sharding import PartitionSpec as P

wave_scale = 0.35 / 64.0
sine_terms = (
    0.9999999970821931,
    -0.6449338560287435,
    0.1668058873098644,
    -0.023932847910373648,
    0.0021836636774330933,
    -0.00012284698513521545,
)
period_shift = 1.5 * 2.0**24
axes = ("row", "col")
POINT_ROWS = 16
BOUND_ROW = 132


def coherence(left_points, right_points):
    difference = (left_points[:, :, None] - right_points[:, None, :]).astype(jnp.float32)
    squared = jnp.sum(difference * difference, axis=0)
    return jnp.sinc(wave_scale * jnp.sqrt(squared)).astype(jnp.bfloat16)


def split_parts(matrix):
    high_part = matrix.astype(jnp.bfloat16)
    low_part = (matrix - high_part.astype(jnp.float32)).astype(jnp.bfloat16)
    return (high_part, low_part)


def modal_product(node_shapes, node_projection):
    high_part, low_part = split_parts(node_projection)
    dims = (((1,), (1,)), ((), ()))
    upper = lax.dot_general(node_shapes, high_part, dims, preferred_element_type=jnp.float32)
    lower = lax.dot_general(node_shapes, low_part, dims, preferred_element_type=jnp.float32)
    return upper + lower


def local_general(coords, mode_shapes, output_shapes, response_gain):
    row_shapes = lax.all_gather(mode_shapes, "col", axis=1, tiled=True)
    row_points = lax.all_gather(coords, "col", axis=1, tiled=True)
    mode_count = mode_shapes.shape[0]
    piece_shapes = lax.all_gather(mode_shapes, "row", axis=1, tiled=True)
    piece_points = lax.all_gather(coords, "row", axis=1, tiled=True)
    length = piece_shapes.shape[1]
    block_size = math.gcd(length, 1024)

    def add_block(loop_index, running_sum):
        block_start = loop_index * block_size
        part_shapes = lax.dynamic_slice_in_dim(piece_shapes, block_start, block_size, 1)
        part_points = lax.dynamic_slice_in_dim(piece_points, block_start, block_size, 1)
        tile = coherence(part_points, row_points)
        return running_sum + jnp.dot(part_shapes, tile, preferred_element_type=jnp.float32)

    zero_block = jnp.zeros((mode_count, row_points.shape[1]), jnp.float32)
    projection = lax.fori_loop(0, length // block_size, add_block, zero_block)
    modal_csd = lax.psum(modal_product(row_shapes, projection), axes)
    real_part, imag_part = response_gain[0], response_gain[1]
    gains = real_part[:, None] * real_part[None, :] + imag_part[:, None] * imag_part[None, :]
    weighted_high, weighted_low = split_parts(gains * modal_csd)
    mapped = jnp.dot(output_shapes, weighted_high, preferred_element_type=jnp.float32)
    mapped = mapped + jnp.dot(output_shapes, weighted_low, preferred_element_type=jnp.float32)
    response_power = jnp.sum(mapped * output_shapes.astype(jnp.float32), axis=1)
    return (response_power, modal_csd)


BIT_X, BIT_Y, BIT_Z, BIT_W = 1, 2, 4, 8
CHIP_AT = (13, 12, 7, 6, 10, 11, 1, 0, 14, 15, 4, 5, 9, 8, 2, 3)
OFFSET_A = ((0, 1), (3, 0))
OFFSET_B = ((2, 0), (4, 1))


def moved(place, offset):
    return (place[0] + offset[0]) % 8, (place[1] + offset[1]) % 2


def partner(chip, offset):
    place = CHIP_AT.index(chip)
    i, j = moved((place // 2, place % 2), offset)
    return CHIP_AT[2 * i + j]


def share(left, right):
    shares = []
    for l, r in zip(left, right):
        difference = (r[0] - l[0]) % 8, (r[1] - l[1]) % 2
        shares.append(0.5 if moved(difference, difference) == (0, 0) else 1.0)
    return tuple(shares)


ROLE_S = ((0, 0), (0, 0))
ROLE_A, ROLE_B, ROLE_E = OFFSET_A, OFFSET_B, OFFSET_A[::-1]


def receive(array, source):
    count = lax.axis_size(axes)
    pairs = []
    for device in range(count):
        chip, core = source(device >> 1, device & 1)
        pairs.append((chip * 2 + core, device))
    return lax.ppermute(array, axes, pairs)


def other_core(array):
    return receive(array, lambda chip, core: (chip, 1 - core))


def column_points(block):
    rows = block[256 : 256 + POINT_ROWS, :].astype(jnp.float32)
    points = rows[0:8, :] * 256.0 + rows[8:16, :]
    columns = jnp.transpose(points, (1, 0))
    return [columns[:, k : k + 1] for k in range(3)]


def row_points(block):
    rows = block[256 : 256 + POINT_ROWS, :].astype(jnp.float32)
    points = rows[0:8, :] * 256.0 + rows[8:16, :]
    return [points[k : k + 1, :] for k in range(3)]


def coherence_tile(columns, rows):
    squared = None
    for column, row in zip(columns, rows):
        difference = column - row
        term = difference * difference
        squared = term if squared is None else squared + term
    squared = jnp.maximum(squared, 1e-6)
    inverse = lax.rsqrt(squared)
    x = squared * (inverse * wave_scale)
    r = x - ((x + period_shift) - period_shift)
    z = r * r
    scale = 1.0 / wave_scale
    q = jnp.full_like(z, sine_terms[-1] * scale)
    for term in sine_terms[-2::-1]:
        q = q * z + term * scale
    return ((r * (1.0 - z)) * (q * inverse)).astype(jnp.bfloat16)


def dot(a, b):
    return jnp.dot(a, b, preferred_element_type=jnp.float32)


def dot_t(a, b):
    return lax.dot_general(a, b, (((1,), (1,)), ((), ())), preferred_element_type=jnp.float32)


def beside(*arrays):
    return jnp.concatenate(arrays, axis=1)


def shapes_of(block):
    return block[0:256, :]


def projection(left_halves, right_half):
    right = row_points(right_half)
    tiles = [coherence_tile(column_points(half), right) for half in left_halves]
    return dot(beside(*[shapes_of(half) for half in left_halves]), jnp.concatenate(tiles, axis=0))


def projection_t(left_halves, right_half):
    right = column_points(right_half)
    tiles = [coherence_tile(right, row_points(half)) for half in left_halves]
    return dot_t(beside(*[shapes_of(half) for half in left_halves]), beside(*tiles))


def modal(projections, right_halves):
    return dot_t(
        beside(*[p.astype(jnp.bfloat16) for p in projections]), beside(*[shapes_of(half) for half in right_halves])
    )


def this_core():
    return lax.axis_index("col") & 1


def shared(left, right, value):
    on_0, on_1 = share(left, right)
    if on_0 == on_1:
        return value if on_0 == 1.0 else on_0 * value
    return jnp.where(this_core() == 0, on_0, on_1).astype(jnp.float32) * value


def early_kernel(own, a, response_gain, out, gains):
    gains[...] = response_gain[...]
    pairs = [shared(ROLE_S, ROLE_A, projection([own[0], own[1]], a[k])) for k in range(2)]
    pairs.append(0.5 * projection([own[0], own[1]], own[0]))
    out[...] = modal(pairs, [a[0], a[1], own[0]])


def late_kernel(own, a, b, e0, e1, early, out):
    pairs = [
        shared(ROLE_S, ROLE_B, projection_t([own[0], own[1]], b[k]))
        + shared(ROLE_A, ROLE_B, projection_t([a[0], a[1]], b[k]))
        + shared(ROLE_E, ROLE_B, projection_t([e0[...], e1[...]], b[k]))
        for k in range(2)
    ]
    core = this_core()
    pairs += [shared(ROLE_A, ROLE_E, projection_t([a[i]], e)) for i, e in ((core, e0[...]), (1 - core, e1[...]))]
    total = early[...] + modal(pairs, [b[0], b[1], e0[...], e1[...]])
    first = total[0:128, 0:128] + total[0:128, 0:128].T
    second = total[128:256, 128:256] + total[128:256, 128:256].T
    cross = total[0:128, 128:256] + total[128:256, 0:128].T
    r = lax.broadcasted_iota(jnp.int32, (128, 128), 0)
    s = lax.broadcasted_iota(jnp.int32, (128, 128), 1)
    corner = jnp.where(r <= s, first, second)
    out[0:128, 0:128] = corner
    out[0:128, 128:256] = cross
    diagonal = jnp.sum(jnp.where(r == s, second, 0.0), axis=0, keepdims=True)
    out[128:BOUND_ROW, :] = jnp.broadcast_to(beside(diagonal, diagonal), (4, 256))
    largest = jnp.maximum(jnp.max(jnp.abs(beside(corner, cross)), axis=0, keepdims=True), jnp.abs(beside(diagonal, diagonal)))
    out[BOUND_ROW:, :] = jnp.broadcast_to(largest, (out.shape[0] - BOUND_ROW, 256))


def answer_kernel(total, gains, outputs_t, power, csd):
    packed = total[...]
    r = lax.broadcasted_iota(jnp.int32, (128, 128), 0)
    s = lax.broadcasted_iota(jnp.int32, (128, 128), 1)
    corner = packed[0:128, 0:128]
    turned = corner.T
    diagonal = packed[128:129, 0:128]
    first = jnp.where(r <= s, corner, turned)
    second = jnp.where(r > s, corner, jnp.where(r == s, diagonal, turned))
    cross = packed[0:128, 128:256]
    whole = jnp.concatenate([beside(first, cross), beside(cross.T, second)], axis=0)
    csd[...] = whole
    g = gains[...]
    columns = jnp.transpose(g, (1, 0))
    weight = columns[:, 0:1] * g[0:1, :] + columns[:, 1:2] * g[1:2, :]
    weighted = (weight * whole).astype(jnp.bfloat16)
    width = 512
    for k in range(outputs_t.shape[1] // width):
        part = outputs_t[:, k * width : (k + 1) * width]
        mapped = dot(weighted, part)
        power[:, k * width : (k + 1) * width] = jnp.sum(mapped * part.astype(jnp.float32), axis=0, keepdims=True)


VMEM = pl.BlockSpec(memory_space=pltpu.VMEM)


def call(kernel, specs, outs, *operands):
    return pl.pallas_call(
        kernel,
        in_specs=specs,
        out_specs=[VMEM] * len(outs) if len(outs) > 1 else VMEM,
        out_shape=outs if len(outs) > 1 else outs[0],
        compiler_params=pltpu.CompilerParams(vmem_limit_bytes=24 * 2**20),
    )(*operands)


def four_chips(sent, first, second):
    core = lax.axis_index("col") & 1
    half = 72
    rest = sent.shape[0] - half
    far = receive(sent, lambda chip, c: (chip ^ (second if c == 0 else first ^ second), c))
    part = lax.dynamic_slice_in_dim(sent, core * rest, half, 0)
    near = receive(part, lambda chip, c: (chip ^ first, c))
    far_other = other_core(far)
    near_other = other_core(near)
    near_all = jnp.where(
        core == 0,
        jnp.concatenate([near[:rest], near_other], axis=0),
        jnp.concatenate([near_other[:rest], near], axis=0),
    )
    return near_all, far, far_other


def scaled(packed):
    exponent = jnp.clip(jnp.round(jnp.log2(packed[BOUND_ROW : BOUND_ROW + 1])), -100.0, 100.0)
    row = lax.broadcasted_iota(jnp.int32, packed.shape, 0)
    return jnp.where(row < BOUND_ROW, packed * jnp.exp2(-exponent), exponent).astype(jnp.float16)


def unscaled(sent):
    wide = sent.astype(jnp.float32)
    return wide * jnp.exp2(wide[BOUND_ROW : BOUND_ROW + 1])


def pack(mode_shapes, coords):
    modes = mode_shapes.shape[0]
    high, low = (coords >> 8).astype(jnp.bfloat16), (coords & 255).astype(jnp.bfloat16)
    return (
        jnp.pad(mode_shapes, ((0, POINT_ROWS), (0, 0)))
        + jnp.pad(high, ((modes, POINT_ROWS - 3), (0, 0)))
        + jnp.pad(low, ((modes + 8, POINT_ROWS - 11), (0, 0)))
    )


def local_chips(coords, mode_shapes, output_shapes, response_gain):
    modes, nodes = mode_shapes.shape
    packed = pack(mode_shapes, coords)
    own = jnp.stack([packed, pack(other_core(mode_shapes), other_core(coords))])
    a = receive(own, lambda chip, c: (partner(chip, OFFSET_A[c]), c))
    b = receive(own, lambda chip, c: (partner(chip, OFFSET_B[c]), c))
    e0, e1 = other_core(a[0]), other_core(a[1])
    square = jax.ShapeDtypeStruct((modes, modes), jnp.float32)
    tri = jax.ShapeDtypeStruct((modes // 2 + 8, modes), jnp.float32)
    gain_rows = jax.ShapeDtypeStruct(response_gain.shape, jnp.float32)
    early, gains = call(early_kernel, [VMEM] * 3, [square, gain_rows], own, a, response_gain)
    mine = call(late_kernel, [VMEM] * 6, [tri], own, a, b, e0, e1, early)
    chip_sum = mine + other_core(mine)
    f = jnp.float32
    sent = chip_sum.astype(jnp.bfloat16)
    pa, pb, pc = four_chips(sent, BIT_Z, BIT_W)
    line_sum = (sent.astype(f) + pa.astype(f)) + (pb.astype(f) + pc.astype(f))
    sent = scaled(line_sum)
    pa, pb, pc = four_chips(sent, BIT_X, BIT_Y)
    total = (unscaled(sent) + unscaled(pa)) + (unscaled(pb) + unscaled(pc))
    count = output_shapes.shape[0]
    power, csd = call(
        answer_kernel,
        [VMEM] * 3,
        [jax.ShapeDtypeStruct((1, count), jnp.float32), square],
        total,
        gains,
        output_shapes.T,
    )
    return (power.reshape(count), csd)


def solution(mesh):
    in_specs = (P(None, axes), P(None, axes), P(axes, None), P())
    out_specs = (P(axes), P())

    def whole(coords, mode_shapes, output_shapes, response_gain):
        shape = (mode_shapes.shape[0], mode_shapes.shape[1] // mesh.size)
        chips = mesh.shape["row"] == 8 and mesh.shape["col"] == 4 and shape == (256, 128)
        local = local_chips if chips else local_general
        return jax.shard_map(local, mesh=mesh, in_specs=in_specs, out_specs=out_specs, check_vma=False)(
            coords, mode_shapes, output_shapes, response_gain
        )

    return whole
```
